32 devices in a mesh: ctx: 8 (over z, x), tp: 4 (over y, core).
Axes of the slice: x: 2, y: 2, z: 4, core: 2. Of those that a mesh axis runs over, the one named last changes fastest.
Arguments:
- query_in: bfloat16 [12288, 8192], P('ctx', 'tp'), may hold values from -6 to 6
- key_in: bfloat16 [12288, 8192], P('ctx', 'tp'), may hold values from -6 to 6
- value_in: bfloat16 [12288, 8192], P('ctx', 'tp'), may hold values from -6 to 6
- cotangent: bfloat16 [12288, 8192], P('ctx', 'tp'), may hold values from -14 to 14
- filter_taps: float32 [512, 128], P('tp'), may hold values from -1 to 1
Outputs:
- query_grad: bfloat16 [12288, 8192], P('ctx', 'tp')
- key_grad: bfloat16 [12288, 8192], P('ctx', 'tp')
- value_grad: bfloat16 [12288, 8192], P('ctx', 'tp')
- filter_grad: float32 [512, 128], P('tp')
The draws below stay inside these ranges and needn't reach their ends.
All inputs are finite; a program needn't handle non-finite values.
Results may differ from the reference program's by a relative error of at most 0.0059.
Values may be sent and summed in bfloat16 or wider, within the bound.
No kernel may reach another device: no remote copies, remote signals or barrier semaphores. Data moves between devices by JAX's collectives and lax.ppermute only.
A program may use at most 256 MiB of HBM per device.

```python
import math
import jax
import jax.numpy as jnp
from jax import lax

D = 8192
GROUP = 16
TAPS = 128
TOKENS = 12288
GROUPS = 512


def draw_cotangent(key, part):
    key = jax.random.fold_in(key, 12)
    row_scale = 0.5 + jnp.arange(TOKENS, dtype=jnp.float32)[:, None] / TOKENS
    col_scale = 0.5 + jnp.arange(D, dtype=jnp.float32)[None, :] / D
    values = jax.random.truncated_normal(key, -4.0, 4.0, (TOKENS, D), jnp.float32) * row_scale * col_scale * 1.5
    return values.astype(jnp.bfloat16)


def draw_filter_taps(key, part):
    key = jax.random.fold_in(key, 11)
    log_rate = jax.random.uniform(jax.random.fold_in(key, 3), (GROUPS, 1), jnp.float32, math.log(0.003), math.log(0.08))
    decay = jnp.exp(-jnp.exp(log_rate) * jnp.arange(TAPS, dtype=jnp.float32)[None, :])
    base = jax.random.truncated_normal(key, -5.0, 5.0, (GROUPS, TAPS), jnp.float32)
    return base * 0.15 * decay


def shard_levels(rng, shape, cuts, least, top_value):
    def one(position, blocks):
        heights = jax.random.uniform(jax.random.fold_in(jax.random.fold_in(rng, 6), position), (blocks,), jnp.float32, least / len(cuts), top_value / len(cuts))
        return jnp.repeat(jnp.exp(heights), shape[position] // blocks).reshape((-1,) + (1,) * (len(shape) - position - 1))

    level = one(*cuts[0])
    for cut in cuts[1:]:
        level = level * one(*cut)
    return level


def centred(own_key, dims, scale, reach, split=(), kind=jnp.bfloat16):
    gain = shard_levels(own_key, dims, split, -0.22, 0.18) if split else 1.0
    values = jax.random.normal(own_key, dims, jnp.float32) * scale * gain
    return jnp.minimum(jnp.maximum(values, -reach), reach).astype(kind)


def setup_inputs(seed: int = 0) -> dict:
    seeds = jax.random.split(jax.random.key(seed), 6)
    return {
        "query_in": centred(seeds[0], (TOKENS, D), 1.0, 6.0, ((0, 8), (1, 4))),
        "key_in": centred(seeds[1], (TOKENS, D), 1.0, 6.0, ((0, 8), (1, 4))),
        "value_in": centred(seeds[2], (TOKENS, D), 1.0, 6.0, ((0, 8), (1, 4))),
        "cotangent": draw_cotangent(jax.random.fold_in(seeds[5], 71), 0),
        "filter_taps": draw_filter_taps(jax.random.fold_in(seeds[5], 71), 0),
    }


clip_ratio = 0.25
epsilon = 1e-06

def tap_tables(span):
    tap_idx = lax.broadcasted_iota(jnp.int32, (span, span, span), 0)
    row_idx = lax.broadcasted_iota(jnp.int32, (span, span, span), 1)
    col_idx = lax.broadcasted_iota(jnp.int32, (span, span, span), 2)
    lower_mask = (row_idx - col_idx == tap_idx).astype(jnp.float32)
    upper_mask = (row_idx - col_idx + span == tap_idx).astype(jnp.float32)
    return (lower_mask, upper_mask)

def rounded(values):
    return lax.optimization_barrier(values.astype(jnp.bfloat16)).astype(jnp.float32)

def reference(query_in, key_in, value_in, cotangent, filter_taps):
    high = lax.Precision.HIGHEST
    lower_mask, upper_mask = tap_tables(TAPS)
    taps_round = rounded(filter_taps)
    stretch = GROUP * 8 if D % (GROUP * 8) == 0 else GROUP
    per_stretch = stretch // GROUP
    block_count = TOKENS // TAPS
    block_shape = (block_count, TAPS, per_stretch, GROUP)

    def advance(stretch_id, carry):
        grad_query, grad_key, grad_value, grad_taps = carry
        start = (stretch_id * stretch).astype(jnp.int32)

        def take(array):
            return lax.dynamic_slice_in_dim(array, start, stretch, 1).astype(jnp.float32)
        queries, keys, values, cotan = (take(query_in), take(key_in), take(value_in), take(cotangent))
        filt = lax.dynamic_slice_in_dim(taps_round, (stretch_id * per_stretch).astype(jnp.int32), per_stretch, 0)
        a_low = jnp.einsum('gt,tij->gij', filt, lower_mask, precision=high)
        a_up = jnp.einsum('gt,tij->gij', filt, upper_mask, precision=high)
        blocked = rounded(keys * values).reshape(block_shape)
        earlier = jnp.concatenate([jnp.zeros((1,) + block_shape[1:], jnp.float32), blocked[:-1]], 0)
        conv = jnp.einsum('gij,bjgc->bigc', a_low, blocked, precision=high) + jnp.einsum('gij,bjgc->bigc', a_up, earlier, precision=high)
        conv = conv.reshape(TOKENS, stretch)
        sig_blocks = rounded(cotan * queries).reshape(block_shape)
        later = jnp.concatenate([sig_blocks[1:], jnp.zeros((1,) + block_shape[1:], jnp.float32)], 0)
        back = jnp.einsum('gij,bigc->bjgc', a_low, sig_blocks, precision=high) + jnp.einsum('gij,bigc->bjgc', a_up, later, precision=high)
        back = back.reshape(TOKENS, stretch)
        same_block = jnp.einsum('bigc,bjgc->gij', sig_blocks, blocked, precision=high)
        cross_block = jnp.einsum('bigc,bjgc->gij', sig_blocks, earlier, precision=high)
        part_grad = jnp.einsum('gij,tij->gt', same_block, lower_mask, precision=high) + jnp.einsum('gij,tij->gt', cross_block, upper_mask, precision=high)
        grad_query = lax.dynamic_update_slice_in_dim(grad_query, (cotan * conv).astype(jnp.bfloat16), start, 1)
        grad_key = lax.dynamic_update_slice_in_dim(grad_key, (back * values).astype(jnp.bfloat16), start, 1)
        grad_value = lax.dynamic_update_slice_in_dim(grad_value, (back * keys).astype(jnp.bfloat16), start, 1)
        grad_taps = lax.dynamic_update_slice_in_dim(grad_taps, part_grad, (stretch_id * per_stretch).astype(jnp.int32), 0)
        return (grad_query, grad_key, grad_value, grad_taps)
    empty = jnp.zeros((TOKENS, D), jnp.bfloat16)
    carry = (empty, empty, empty, jnp.zeros((GROUPS, TAPS), jnp.float32))
    grad_query, grad_key, grad_value, grad_taps = lax.fori_loop(0, D // stretch, advance, carry)
    scaled = grad_taps * (1.0 / math.sqrt(TOKENS * GROUP))
    norm_value = jnp.sqrt(jnp.sum(scaled * scaled) + epsilon)
    factor = jnp.minimum(1.0, clip_ratio * math.sqrt(GROUPS * TAPS) / norm_value)
    return (grad_query, grad_key, grad_value, scaled * factor)
```

```python
import math

import jax
import jax.numpy as jnp
from jax import lax
from jax.experimental import pallas as pl
from jax.experimental.pallas import tpu as pltpu
from jax.sharding import PartitionSpec as P

clip_ratio = 0.25
epsilon = 1e-06
LANES = 128
TILE = 16
WIDE = 256
bf16 = jnp.bfloat16
f32 = jnp.float32


def shifted(value, axis, steps):
    count = lax.axis_size(axis)
    first, last = max(0, -steps), min(count, count - steps)
    return lax.ppermute(value, axis, [(source, source + steps) for source in range(first, last)])


def butterfly(value, axis):
    count, step = lax.axis_size(axis), 1
    while step < count:
        value = value + lax.ppermute(value, axis, [(i, i ^ step) for i in range(count)])
        step *= 2
    return value


def toeplitz(tap):
    lane = lax.broadcasted_iota(jnp.int32, (TILE, LANES), 1)
    row = lax.broadcasted_iota(jnp.int32, (TILE, LANES), 0)
    zero = jnp.zeros((TILE, LANES), bf16)
    tap = jnp.broadcast_to(tap.astype(bf16).astype(f32), (TILE, LANES))
    first = pltpu.roll(tap, 0, 1, stride=1, stride_axis=0).astype(bf16)
    upper, lower = [], []
    for a in range(LANES // TILE):
        rows = pltpu.roll(first, a * TILE, 1) if a else first
        keep = lane >= row + a * TILE
        upper.append(jnp.where(keep, rows, zero))
        lower.append(jnp.where(keep, zero, rows))
    return jnp.concatenate(upper, 0), jnp.concatenate(lower, 0)


def diagonal_sums(folded, groups):
    total = jnp.zeros((groups * TILE, LANES), f32)
    source = lax.broadcasted_iota(jnp.int32, (LANES, LANES), 0)
    target = lax.broadcasted_iota(jnp.int32, (LANES, LANES), 1)
    for a in range(0, LANES // TILE, 2):
        left = jnp.concatenate([folded[a], folded[a + 1]], 1)
        right = [((target + TILE * (a + i)) % LANES == source).astype(bf16) for i in range(2)]
        total = total + jnp.dot(left, jnp.concatenate(right, 0), preferred_element_type=f32)
    row = lax.broadcasted_iota(jnp.int32, total.shape, 0)
    for step in (1, 2, 4, 8):
        total = jnp.where(row & step != 0, pltpu.roll(total, LANES - step, 1), total)
    return jnp.sum(total.reshape(groups, TILE, LANES), 1)


def main_body(q_ref, k_ref, v_ref, c_ref, taps_ref, before_ref, after_ref, dq_ref, dk_ref, dv_ref, raw_ref, mt, st, ct, bt, folded):
    length, width = q_ref.shape
    groups = taps_ref.shape[0]
    group = width // groups
    blocks = length // LANES
    lane = lax.broadcasted_iota(jnp.int32, (TILE, LANES), 1)
    row = lax.broadcasted_iota(jnp.int32, (TILE, LANES), 0)
    flat = lambda x: x.reshape(blocks * group, LANES)
    for h in range(width // LANES):
        cols = slice(h * LANES, (h + 1) * LANES)
        mt[h, 0] = before_ref[:, cols].T
        st[h, blocks] = after_ref[:, cols].T
        for b in range(blocks):
            rows = slice(b * LANES, (b + 1) * LANES)
            mt[h, b + 1] = (k_ref[rows, cols] * v_ref[rows, cols]).T
            st[h, b] = (c_ref[rows, cols] * q_ref[rows, cols]).T
        for p in range(LANES // group):
            g = h * (LANES // group) + p
            own = slice(p * group, (p + 1) * group)
            upper, lower = toeplitz(taps_ref[g : g + 1, :])
            mixed = flat(mt[h, 1 : blocks + 1, own, :])
            window = jnp.concatenate([flat(mt[h, :blocks, own, :]), mixed], 1)
            ahead = jnp.concatenate([flat(st[h, :blocks, own, :]), flat(st[h, 1 : blocks + 1, own, :])], 1)
            conv = jnp.dot(window, jnp.concatenate([lower, upper], 0), preferred_element_type=f32)
            back = lax.dot_general(ahead, jnp.concatenate([upper, lower], 1), (((1,), (1,)), ((), ())), preferred_element_type=f32)
            ct[h, :, own, :] = conv.astype(bf16).reshape(blocks, group, LANES)
            bt[h, :, own, :] = back.astype(bf16).reshape(blocks, group, LANES)
            gram = lax.dot_general(mixed, ahead, (((0,), (0,)), ((), ())), preferred_element_type=f32)
            for a in range(LANES // TILE):
                rows = slice(a * TILE, (a + 1) * TILE)
                kept = jnp.where(lane >= row + a * TILE, gram[rows, :LANES], gram[rows, LANES:])
                folded[a, g * TILE : (g + 1) * TILE, :] = kept.astype(bf16)
        for b in range(blocks):
            rows = slice(b * LANES, (b + 1) * LANES)
            dq_ref[rows, cols] = c_ref[rows, cols] * ct[h, b].T
            back = bt[h, b].T
            dk_ref[rows, cols] = v_ref[rows, cols] * back
            dv_ref[rows, cols] = k_ref[rows, cols] * back
    raw_ref[...] = diagonal_sums(folded, groups)


def main_part(q, k, v, c, taps, before, after):
    length, width = q.shape
    local_groups, span = taps.shape
    groups = WIDE * local_groups // width
    blocks, halves = length // LANES, WIDE // LANES
    block = pl.BlockSpec((length, WIDE), lambda i: (0, i))
    halo = pl.BlockSpec((span, WIDE), lambda i: (0, i))
    some = pl.BlockSpec((groups, span), lambda i: (i, 0))
    big = jax.ShapeDtypeStruct((length, width), bf16)
    return pl.pallas_call(
        main_body,
        grid=(width // WIDE,),
        in_specs=[block] * 4 + [some, halo, halo],
        out_specs=[block] * 3 + [some],
        out_shape=[big, big, big, jax.ShapeDtypeStruct((local_groups, span), f32)],
        scratch_shapes=[pltpu.VMEM((halves, blocks + 1, LANES, LANES), bf16)] * 2
        + [pltpu.VMEM((halves, blocks, LANES, LANES), bf16)] * 2
        + [pltpu.VMEM((LANES // TILE, groups * TILE, LANES), bf16)],
        compiler_params=pltpu.CompilerParams(vmem_limit_bytes=48 << 20),
    )(q, k, v, c, taps, before, after)


def on_device(query_in, key_in, value_in, cotangent, filter_taps):
    length, width = query_in.shape
    local_groups, span = filter_taps.shape
    group_size = width // local_groups
    after = shifted(cotangent[:span] * query_in[:span], "ctx", -1)
    before = shifted(key_in[length - span :] * value_in[length - span :], "ctx", 1)
    query_grad, key_grad, value_grad, raw = main_part(query_in, key_in, value_in, cotangent, filter_taps, before, after)
    inverse = 1.0 / math.sqrt(length * lax.axis_size("ctx") * group_size)
    limit = clip_ratio * math.sqrt(local_groups * lax.axis_size("tp") * span)
    scaled = butterfly(raw, "ctx") * inverse
    squares = butterfly(jnp.broadcast_to(jnp.sum(scaled * scaled), (8, LANES)), "tp")[0, 0]
    factor = jnp.minimum(1.0, limit / jnp.sqrt(squares + epsilon))
    return (query_grad, key_grad, value_grad, scaled * factor)


def solution(mesh):
    placed = (P("ctx", "tp"), P("ctx", "tp"), P("ctx", "tp"), P("ctx", "tp"), P("tp", None))
    return jax.shard_map(
        on_device,
        mesh=mesh,
        in_specs=placed,
        out_specs=(P("ctx", "tp"), P("ctx", "tp"), P("ctx", "tp"), P("tp", None)),
        check_vma=False,
    )
```

```python
import math

import jax
import jax.numpy as jnp
from jax import lax
from jax.experimental import pallas as pl
from jax.experimental.pallas import tpu as pltpu
from jax.sharding import PartitionSpec as P

clip_ratio = 0.25
epsilon = 1e-06
LANES = 128
TILE = 16
WIDE = 256
VMEM = 60 << 20
EDGE_VMEM = 61 << 20
bf16 = jnp.bfloat16
f32 = jnp.float32


def shifted(value, axis, steps):
    count = lax.axis_size(axis)
    first, last = max(0, -steps), min(count, count - steps)
    return lax.ppermute(value, axis, [(source, source + steps) for source in range(first, last)])


def partners(value, masks):
    across, along = lax.axis_size("ctx"), lax.axis_size("tp")
    numbers = range(across * along)
    return [lax.ppermute(value, ("ctx", "tp"), [(i, i ^ (c * along + t)) for i in numbers]) for c, t in masks]


def summed(value, received):
    if len(received) == 1:
        return value + received[0]
    return (value + received[0]) + (received[1] + received[2])


def rounds(bits):
    out = []
    while bits:
        a, b, bits = bits[0], bits[1] if len(bits) > 1 else 0, bits[2:]
        out.append([a, b, a ^ b] if b else [a])
    return out


def powers(lowest, count):
    out = []
    while lowest < count:
        out.append(lowest)
        lowest *= 2
    return out


def toeplitz(tap):
    lane = lax.broadcasted_iota(jnp.int32, (TILE, LANES), 1)
    row = lax.broadcasted_iota(jnp.int32, (TILE, LANES), 0)
    zero = jnp.zeros((TILE, LANES), bf16)
    tap = jnp.broadcast_to(tap.astype(bf16).astype(f32), (TILE, LANES))
    first = pltpu.roll(tap, 0, 1, stride=1, stride_axis=0).astype(bf16)
    upper, lower = [], []
    for a in range(LANES // TILE):
        rows = pltpu.roll(first, a * TILE, 1) if a else first
        keep = lane >= row + a * TILE
        upper.append(jnp.where(keep, rows, zero))
        lower.append(jnp.where(keep, zero, rows))
    return jnp.concatenate(upper, 0), jnp.concatenate(lower, 0)


def diagonal_sums(folded, groups):
    total = jnp.zeros((groups * TILE, LANES), f32)
    source = lax.broadcasted_iota(jnp.int32, (LANES, LANES), 0)
    target = lax.broadcasted_iota(jnp.int32, (LANES, LANES), 1)
    for a in range(0, LANES // TILE, 2):
        left = jnp.concatenate([folded[a], folded[a + 1]], 1)
        right = [((source + target) % LANES == TILE * (a + i)).astype(bf16) for i in range(2)]
        total = total + jnp.dot(left, jnp.concatenate(right, 0), preferred_element_type=f32)
    sums = []
    for g in range(groups):
        part = pltpu.roll(total[g * TILE : (g + 1) * TILE], 0, 1, stride=1, stride_axis=0)
        sums.append(jnp.sum(part, 0, keepdims=True))
    return jnp.concatenate(sums, 0)


def main_body(q_ref, k_ref, v_ref, c_ref, taps_ref, dq_ref, dk_ref, dv_ref, folded, first_ref, last_ref, lower_ref, mt, st, ct, bt):
    length, width = q_ref.shape
    groups = taps_ref.shape[0]
    group = width // groups
    blocks = length // LANES
    lane = lax.broadcasted_iota(jnp.int32, (TILE, LANES), 1)
    row = lax.broadcasted_iota(jnp.int32, (TILE, LANES), 0)
    flat = lambda x: x.reshape(blocks * group, LANES)
    for h in range(width // LANES):
        cols = slice(h * LANES, (h + 1) * LANES)
        mt[h, 0] = jnp.zeros((LANES, LANES), bf16)
        st[h, blocks] = jnp.zeros((LANES, LANES), bf16)
        for b in range(blocks):
            rows = slice(b * LANES, (b + 1) * LANES)
            mt[h, b + 1] = (k_ref[rows, cols] * v_ref[rows, cols]).T
            st[h, b] = (c_ref[rows, cols] * q_ref[rows, cols]).T
        for p in range(LANES // group):
            g = h * (LANES // group) + p
            own = slice(p * group, (p + 1) * group)
            upper, lower = toeplitz(taps_ref[g : g + 1, :])
            lower_ref[g] = lower
            mixed = flat(mt[h, 1 : blocks + 1, own, :])
            window = jnp.concatenate([flat(mt[h, :blocks, own, :]), mixed], 1)
            ahead = jnp.concatenate([flat(st[h, :blocks, own, :]), flat(st[h, 1 : blocks + 1, own, :])], 1)
            conv = jnp.dot(window, jnp.concatenate([lower, upper], 0), preferred_element_type=f32)
            back = lax.dot_general(ahead, jnp.concatenate([upper, lower], 1), (((1,), (1,)), ((), ())), preferred_element_type=f32)
            ct[h, :, own, :] = conv.astype(bf16).reshape(blocks, group, LANES)
            bt[h, :, own, :] = back.astype(bf16).reshape(blocks, group, LANES)
            gram = lax.dot_general(mixed, ahead, (((0,), (0,)), ((), ())), preferred_element_type=f32)
            for a in range(LANES // TILE):
                rows = slice(a * TILE, (a + 1) * TILE)
                kept = jnp.where(lane >= row + a * TILE, gram[rows, :LANES], gram[rows, LANES:])
                folded[a, g * TILE : (g + 1) * TILE, :] = kept.astype(bf16)
        for b in range(blocks):
            rows = slice(b * LANES, (b + 1) * LANES)
            conv = ct[h, b].T
            back = bt[h, b].T
            if b == 0:
                first_ref[:, cols] = conv
            if b == blocks - 1:
                last_ref[:, cols] = back
            dq_ref[rows, cols] = c_ref[rows, cols] * conv
            dk_ref[rows, cols] = v_ref[rows, cols] * back
            dv_ref[rows, cols] = k_ref[rows, cols] * back


def main_part(q, k, v, c, taps):
    length, width = q.shape
    local_groups, span = taps.shape
    groups = WIDE * local_groups // width
    blocks, halves = length // LANES, WIDE // LANES
    block = pl.BlockSpec((length, WIDE), lambda i: (0, i))
    halo = pl.BlockSpec((span, WIDE), lambda i: (0, i))
    some = pl.BlockSpec((groups, span), lambda i: (i, 0))
    big = jax.ShapeDtypeStruct((length, width), bf16)
    edge = jax.ShapeDtypeStruct((span, width), bf16)
    return pl.pallas_call(
        main_body,
        grid=(width // WIDE,),
        in_specs=[block] * 4 + [some],
        out_specs=[block] * 3 + [pl.BlockSpec((span // TILE, groups * TILE, span), lambda i: (0, i, 0)), halo, halo, pl.BlockSpec((groups, span, span), lambda i: (i, 0, 0))],
        out_shape=[big, big, big, jax.ShapeDtypeStruct((span // TILE, local_groups * TILE, span), bf16), edge, edge, jax.ShapeDtypeStruct((local_groups, span, span), bf16)],
        scratch_shapes=[pltpu.VMEM((halves, blocks + 1, LANES, LANES), bf16)] * 2
        + [pltpu.VMEM((halves, blocks, LANES, LANES), bf16)] * 2,
        compiler_params=pltpu.CompilerParams(vmem_limit_bytes=VMEM),
        cost_estimate=pl.CostEstimate(flops=12 * length * width * LANES, bytes_accessed=14 * length * width, transcendentals=0),
    )(q, k, v, c, taps)


def edge_raw_body(k_ref, v_ref, after_ref, inner_ref, out_ref, folded):
    width = k_ref.shape[1]
    groups = out_ref.shape[0]
    group = width // groups
    lane = lax.broadcasted_iota(jnp.int32, (TILE, LANES), 1)
    row = lax.broadcasted_iota(jnp.int32, (TILE, LANES), 0)
    per = LANES // group
    zero = jnp.zeros((TILE, LANES), bf16)
    for h in range(width // LANES):
        cols = slice(h * LANES, (h + 1) * LANES)
        mixed = k_ref[:, cols] * v_ref[:, cols]
        ahead = after_ref[:, cols].T
        empty = jnp.zeros((group, LANES), bf16)
        for p in range(0, per, 2):
            pick = lambda n: jnp.concatenate([ahead[i * group : (i + 1) * group] if i == n else empty for i in range(per)], 0)
            gram = jnp.dot(mixed, jnp.concatenate([pick(p), pick(p + 1)], 1), preferred_element_type=f32)
            for n in range(2):
                g = h * per + p + n
                at = slice(g * TILE, (g + 1) * TILE)
                for a in range(LANES // TILE):
                    part = gram[a * TILE : (a + 1) * TILE, n * LANES : (n + 1) * LANES].astype(bf16)
                    folded[a, at, :] = inner_ref[a, at, :] + jnp.where(lane < row + a * TILE, part, zero)
    out_ref[...] = diagonal_sums(folded, groups)


def edge_raw(k, v, after, inner, wide):
    length, width = k.shape
    span = inner.shape[2]
    local_groups = inner.shape[1] // TILE
    groups = wide * local_groups // width
    tail = pl.BlockSpec((span, wide), lambda i: (length // span - 1, i))
    halo = pl.BlockSpec((span, wide), lambda i: (0, i))
    return pl.pallas_call(
        edge_raw_body,
        grid=(width // wide,),
        in_specs=[tail, tail, halo, pl.BlockSpec((span // TILE, groups * TILE, span), lambda i: (0, i, 0))],
        out_specs=pl.BlockSpec((groups, span), lambda i: (i, 0)),
        out_shape=jax.ShapeDtypeStruct((local_groups, span), f32),
        scratch_shapes=[pltpu.VMEM((LANES // TILE, groups * TILE, LANES), bf16)],
        compiler_params=pltpu.CompilerParams(vmem_limit_bytes=EDGE_VMEM),
        cost_estimate=pl.CostEstimate(flops=2 * span * span * width, bytes_accessed=14 * span * width, transcendentals=0),
    )(k, v, after, inner)


def edge_terms(halo_ref, lower_ref, h, side):
    group = halo_ref.shape[1] // lower_ref.shape[0]
    per = LANES // group
    far = halo_ref[:, h * LANES : (h + 1) * LANES].T
    parts = []
    for p in range(per):
        dims = (((1,), (side,)), ((), ()))
        parts.append(lax.dot_general(far[p * group : (p + 1) * group], lower_ref[h * per + p], dims, preferred_element_type=f32))
    return jnp.concatenate(parts, 0).astype(bf16).T.astype(f32)


def edge_query_body(before_ref, first_ref, lower_ref, c_ref, dq_in, dq_ref):
    for h in range(c_ref.shape[1] // LANES):
        cols = slice(h * LANES, (h + 1) * LANES)
        conv = first_ref[:, cols].astype(f32) + edge_terms(before_ref, lower_ref, h, 0)
        dq_ref[:, cols] = c_ref[:, cols] * conv.astype(bf16)


def edge_key_body(after_ref, last_ref, lower_ref, k_ref, v_ref, dk_in, dv_in, dk_ref, dv_ref):
    for h in range(k_ref.shape[1] // LANES):
        cols = slice(h * LANES, (h + 1) * LANES)
        back = (last_ref[:, cols].astype(f32) + edge_terms(after_ref, lower_ref, h, 1)).astype(bf16)
        dk_ref[:, cols] = v_ref[:, cols] * back
        dv_ref[:, cols] = k_ref[:, cols] * back


def edge_outputs(body, tail, halo, inner, lower, factors, grads, wide):
    length, width = grads[0].shape
    span = lower.shape[1]
    place = length // span - 1 if tail else 0
    head = pl.BlockSpec((span, wide), lambda i: (0, i))
    edge = pl.BlockSpec((span, wide), lambda i: (place, i))
    some = pl.BlockSpec((wide * lower.shape[0] // width, span, span), lambda i: (i, 0, 0))
    count, ahead = len(grads), 3 + len(factors)
    return pl.pallas_call(
        body,
        grid=(width // wide,),
        in_specs=[head, head, some] + [edge] * len(factors) + [pl.BlockSpec(memory_space=pl.ANY)] * count,
        out_specs=[edge] * count,
        out_shape=[jax.ShapeDtypeStruct(g.shape, bf16) for g in grads],
        input_output_aliases={ahead + i: i for i in range(count)},
        compiler_params=pltpu.CompilerParams(vmem_limit_bytes=EDGE_VMEM),
        cost_estimate=pl.CostEstimate(flops=2 * span * span * width, bytes_accessed=12 * span * width, transcendentals=0),
    )(halo, inner, lower, *factors, *grads)


def norm_body(inverse, own_ref, *refs):
    out_ref, squares_ref = refs[-2:]
    own = (own_ref[...] + refs[0][...]) * inverse
    total = jnp.sum(own * own)
    if len(refs) == 5:
        other = (refs[1][...] + refs[2][...]) * inverse
        total = total + jnp.sum(other * other)
    out_ref[...] = own
    squares_ref[...] = jnp.full(squares_ref.shape, total, f32)


def scale_body(limit, scaled_ref, *refs):
    out_ref = refs[-1]
    squares = refs[0][...]
    for ref in refs[1:-1]:
        squares = squares + ref[...]
    factor = jnp.minimum(1.0, limit / jnp.sqrt(squares[:1] + epsilon))
    flip = (lax.broadcasted_iota(jnp.int32, (LANES, LANES), 0) + lax.broadcasted_iota(jnp.int32, (LANES, LANES), 1)) % LANES == 0
    out_ref[...] = jnp.dot(scaled_ref[...] * factor, flip.astype(f32), precision=lax.Precision.HIGHEST, preferred_element_type=f32)


def small_call(body, out_shape, *args):
    return pl.pallas_call(body, out_shape=out_shape, compiler_params=pltpu.CompilerParams(vmem_limit_bytes=8 << 20))(*args)


def on_device(query_in, key_in, value_in, cotangent, filter_taps):
    length, width = query_in.shape
    local_groups, span = filter_taps.shape
    group_size = width // local_groups
    across, along = lax.axis_size("ctx"), lax.axis_size("tp")
    inverse = 1.0 / math.sqrt(length * across * group_size)
    limit = clip_ratio * math.sqrt(local_groups * along * span)
    after = shifted(cotangent[:span] * query_in[:span], "ctx", -1)
    before = shifted(key_in[length - span :] * value_in[length - span :], "ctx", 1)
    query_grad, key_grad, value_grad, inner, first, last, lower = main_part(query_in, key_in, value_in, cotangent, filter_taps)
    wide = min(width, 1024)
    raw = edge_raw(key_in, value_in, after, inner, wide)
    query_grad, = edge_outputs(edge_query_body, False, before, first, lower, [cotangent], [query_grad], wide)
    key_grad, value_grad = edge_outputs(edge_key_body, True, after, last, lower, [key_in, value_in], [key_grad, value_grad], wide)
    for masks in rounds(powers(2, across)):
        received = partners(raw, [(m, 0) for m in masks])
        if masks[0] == 2:
            *received, query_grad = lax.optimization_barrier((*received, query_grad))
        raw = summed(raw, received)
    masks = [(1, 0), (0, 2), (1, 2)] if along > 2 else [(1, 0)]
    shapes = (jax.ShapeDtypeStruct(raw.shape, f32), jax.ShapeDtypeStruct((8, LANES), f32))
    *received, key_grad, value_grad = lax.optimization_barrier((*partners(raw, masks), key_grad, value_grad))
    scaled, squares = small_call(lambda *refs: norm_body(inverse, *refs), shapes, raw, *received)
    steps = [1] + powers(4, along)
    for step in steps[:-1]:
        squares = squares + partners(squares, [(0, step)])[0]
    filter_grad = small_call(lambda *refs: scale_body(limit, *refs), shapes[0], scaled, squares, *partners(squares, [(0, steps[-1])]))
    return (query_grad, key_grad, value_grad, filter_grad)


def solution(mesh):
    placed = (P("ctx", "tp"), P("ctx", "tp"), P("ctx", "tp"), P("ctx", "tp"), P("tp", None))
    return jax.shard_map(
        on_device,
        mesh=mesh,
        in_specs=placed,
        out_specs=(P("ctx", "tp"), P("ctx", "tp"), P("ctx", "tp"), P("tp", None)),
        check_vma=False,
    )
```

```python
import math

import jax
import jax.numpy as jnp
from jax import lax
from jax.experimental import pallas as pl
from jax.experimental.pallas import tpu as pltpu
from jax.sharding import PartitionSpec as P

clip_ratio = 0.25
epsilon = 1e-06
LANES = 128
TILE = 16
WIDE = 256
CHUNK = 2
VMEM = 60 << 20
EDGE_VMEM = 61 << 20
bf16 = jnp.bfloat16
f32 = jnp.float32


def shifted(value, axis, steps):
    count = lax.axis_size(axis)
    first, last = max(0, -steps), min(count, count - steps)
    return lax.ppermute(value, axis, [(source, source + steps) for source in range(first, last)])


def partners(value, masks):
    across, along = lax.axis_size("ctx"), lax.axis_size("tp")
    numbers = range(across * along)
    return [lax.ppermute(value, ("ctx", "tp"), [(i, i ^ (c * along + t)) for i in numbers]) for c, t in masks]


def summed(value, received):
    if len(received) == 1:
        return value + received[0]
    return (value + received[0]) + (received[1] + received[2])


def rounds(bits):
    out = []
    while bits:
        a, b, bits = bits[0], bits[1] if len(bits) > 1 else 0, bits[2:]
        out.append([a, b, a ^ b] if b else [a])
    return out


def powers(lowest, count):
    out = []
    while lowest < count:
        out.append(lowest)
        lowest *= 2
    return out


def toeplitz(tap):
    lane = lax.broadcasted_iota(jnp.int32, (TILE, LANES), 1)
    row = lax.broadcasted_iota(jnp.int32, (TILE, LANES), 0)
    zero = jnp.zeros((TILE, LANES), bf16)
    tap = jnp.broadcast_to(tap.astype(bf16).astype(f32), (TILE, LANES))
    first = pltpu.roll(tap, 0, 1, stride=1, stride_axis=0).astype(bf16)
    upper, lower = [], []
    for a in range(LANES // TILE):
        rows = pltpu.roll(first, a * TILE, 1) if a else first
        keep = lane >= row + a * TILE
        upper.append(jnp.where(keep, rows, zero))
        lower.append(jnp.where(keep, zero, rows))
    return jnp.concatenate(upper, 0), jnp.concatenate(lower, 0)


def diagonal_shifts():
    source = lax.broadcasted_iota(jnp.int32, (LANES, LANES), 0)
    target = lax.broadcasted_iota(jnp.int32, (LANES, LANES), 1)
    return jnp.concatenate([((source + target) % LANES == a).astype(bf16) for a in range(0, LANES, TILE)], 0)


def diagonal_sums(folded, shifts, first, groups):
    at = slice(first * TILE, (first + groups) * TILE)
    left = jnp.concatenate([folded[a, at, :] for a in range(LANES // TILE)], 1)
    total = jnp.dot(left, shifts, preferred_element_type=f32)
    sums = []
    for g in range(groups):
        part = pltpu.roll(total[g * TILE : (g + 1) * TILE], 0, 1, stride=1, stride_axis=0)
        sums.append(jnp.sum(part, 0, keepdims=True))
    return jnp.concatenate(sums, 0)


def main_body(q_ref, k_ref, v_ref, c_ref, taps_ref, dq_ref, dk_ref, dv_ref, folded, first_ref, last_ref, lower_ref, mt, st, ct, bt):
    length, width = q_ref.shape
    groups = taps_ref.shape[0]
    group = width // groups
    blocks = length // LANES
    lane = lax.broadcasted_iota(jnp.int32, (TILE, LANES), 1)
    row = lax.broadcasted_iota(jnp.int32, (TILE, LANES), 0)
    flat = lambda x: x.reshape(blocks * group, LANES)
    per = LANES // group
    halves = width // LANES

    def enter(h, b):
        cols, rows = slice(h * LANES, (h + 1) * LANES), slice(b * LANES, (b + 1) * LANES)
        mixed = k_ref[rows, cols] * v_ref[rows, cols]
        mt[h, b + 1] = mixed.T
        st[h, b] = (c_ref[rows, cols] * q_ref[rows, cols]).T

    def convolve(h, p):
        g = h * per + p
        own = slice(p * group, (p + 1) * group)
        upper, lower = toeplitz(taps_ref[g : g + 1, :])
        lower_ref[g] = lower
        mixed = flat(mt[h, 1 : blocks + 1, own, :])
        window = jnp.concatenate([flat(mt[h, :blocks, own, :]), mixed], 1)
        ahead = jnp.concatenate([flat(st[h, :blocks, own, :]), flat(st[h, 1 : blocks + 1, own, :])], 1)
        conv = jnp.dot(window, jnp.concatenate([lower, upper], 0), preferred_element_type=f32)
        back = lax.dot_general(ahead, jnp.concatenate([upper, lower], 1), (((1,), (1,)), ((), ())), preferred_element_type=f32)
        ct[h, :, own, :] = conv.astype(bf16).reshape(blocks, group, LANES)
        bt[h, :, own, :] = back.astype(bf16).reshape(blocks, group, LANES)
        gram = lax.dot_general(mixed, ahead, (((0,), (0,)), ((), ())), preferred_element_type=f32)
        for a in range(LANES // TILE):
            rows = slice(a * TILE, (a + 1) * TILE)
            kept = jnp.where(lane >= row + a * TILE, gram[rows, :LANES], gram[rows, LANES:])
            folded[a, g * TILE : (g + 1) * TILE, :] = kept.astype(bf16)

    def leave(h, b):
        cols, rows = slice(h * LANES, (h + 1) * LANES), slice(b * LANES, (b + 1) * LANES)
        conv = ct[h, b].T
        back = bt[h, b].T
        if b == 0:
            first_ref[:, cols] = conv
        if b == blocks - 1:
            last_ref[:, cols] = back
        dq_ref[rows, cols] = c_ref[rows, cols] * conv
        dk_ref[rows, cols] = v_ref[rows, cols] * back
        dv_ref[rows, cols] = k_ref[rows, cols] * back

    share = 3
    for h in range(halves):
        mt[h, 0] = jnp.zeros((LANES, LANES), bf16)
        st[h, blocks] = jnp.zeros((LANES, LANES), bf16)
    for b in range(blocks):
        enter(0, b)
    for h in range(halves):
        for p in range(per):
            convolve(h, p)
            for b in range(p * share, min(blocks, (p + 1) * share)):
                if h + 1 < halves:
                    enter(h + 1, b)
                if h > 0:
                    leave(h - 1, b)
    for b in range(blocks):
        leave(halves - 1, b)


def main_part(q, k, v, c, taps):
    length, width = q.shape
    local_groups, span = taps.shape
    groups = WIDE * local_groups // width
    blocks, halves = length // LANES, WIDE // LANES
    block = pl.BlockSpec((length, WIDE), lambda i: (0, i))
    halo = pl.BlockSpec((span, WIDE), lambda i: (0, i))
    some = pl.BlockSpec((groups, span), lambda i: (i, 0))
    big = jax.ShapeDtypeStruct((length, width), bf16)
    edge = jax.ShapeDtypeStruct((span, width), bf16)
    return pl.pallas_call(
        main_body,
        grid=(width // WIDE,),
        in_specs=[block] * 4 + [some],
        out_specs=[block] * 3 + [pl.BlockSpec((span // TILE, groups * TILE, span), lambda i: (0, i, 0)), halo, halo, pl.BlockSpec((groups, span, span), lambda i: (i, 0, 0))],
        out_shape=[big, big, big, jax.ShapeDtypeStruct((span // TILE, local_groups * TILE, span), bf16), edge, edge, jax.ShapeDtypeStruct((local_groups, span, span), bf16)],
        scratch_shapes=[pltpu.VMEM((halves, blocks + 1, LANES, LANES), bf16)] * 2
        + [pltpu.VMEM((halves, blocks, LANES, LANES), bf16)] * 2,
        compiler_params=pltpu.CompilerParams(vmem_limit_bytes=VMEM),
        cost_estimate=pl.CostEstimate(flops=12 * length * width * LANES, bytes_accessed=14 * length * width, transcendentals=0),
    )(q, k, v, c, taps)


def edge_raw_body(k_ref, v_ref, after_ref, inner_ref, out_ref, folded):
    width = k_ref.shape[1]
    groups = out_ref.shape[0]
    group = width // groups
    lane = lax.broadcasted_iota(jnp.int32, (TILE, LANES), 1)
    row = lax.broadcasted_iota(jnp.int32, (TILE, LANES), 0)
    per = LANES // group
    zero = jnp.zeros((TILE, LANES), bf16)
    shifts = diagonal_shifts()
    chunk = CHUNK * per

    def finish(first):
        out_ref[first : first + chunk, :] = diagonal_sums(folded, shifts, first, chunk)

    for h in range(width // LANES):
        cols = slice(h * LANES, (h + 1) * LANES)
        mixed = k_ref[:, cols] * v_ref[:, cols]
        ahead = after_ref[:, cols].T
        empty = jnp.zeros((group, LANES), bf16)
        for p in range(0, per, 2):
            pick = lambda n: jnp.concatenate([ahead[i * group : (i + 1) * group] if i == n else empty for i in range(per)], 0)
            gram = jnp.dot(mixed, jnp.concatenate([pick(p), pick(p + 1)], 1), preferred_element_type=f32)
            for n in range(2):
                g = h * per + p + n
                at = slice(g * TILE, (g + 1) * TILE)
                for a in range(LANES // TILE):
                    part = gram[a * TILE : (a + 1) * TILE, n * LANES : (n + 1) * LANES].astype(bf16)
                    folded[a, at, :] = inner_ref[a, at, :] + jnp.where(lane < row + a * TILE, part, zero)
        if h % CHUNK == 0 and h >= CHUNK:
            finish((h - CHUNK) * per)
    finish(groups - chunk)


def edge_raw(k, v, after, inner, wide):
    length, width = k.shape
    span = inner.shape[2]
    local_groups = inner.shape[1] // TILE
    groups = wide * local_groups // width
    tail = pl.BlockSpec((span, wide), lambda i: (length // span - 1, i))
    halo = pl.BlockSpec((span, wide), lambda i: (0, i))
    return pl.pallas_call(
        edge_raw_body,
        grid=(width // wide,),
        in_specs=[tail, tail, halo, pl.BlockSpec((span // TILE, groups * TILE, span), lambda i: (0, i, 0))],
        out_specs=pl.BlockSpec((groups, span), lambda i: (i, 0)),
        out_shape=jax.ShapeDtypeStruct((local_groups, span), f32),
        scratch_shapes=[pltpu.VMEM((LANES // TILE, groups * TILE, LANES), bf16)],
        compiler_params=pltpu.CompilerParams(vmem_limit_bytes=EDGE_VMEM),
        cost_estimate=pl.CostEstimate(flops=2 * span * span * width, bytes_accessed=14 * span * width, transcendentals=0),
    )(k, v, after, inner)


def edge_terms(halo_ref, lower_ref, h, side):
    group = halo_ref.shape[1] // lower_ref.shape[0]
    per = LANES // group
    far = halo_ref[:, h * LANES : (h + 1) * LANES].T
    parts = []
    for p in range(per):
        dims = (((1,), (side,)), ((), ()))
        parts.append(lax.dot_general(far[p * group : (p + 1) * group], lower_ref[h * per + p], dims, preferred_element_type=f32))
    return jnp.concatenate(parts, 0).astype(bf16).T.astype(f32)


def edge_query_body(before_ref, first_ref, lower_ref, c_ref, dq_in, dq_ref):
    for h in range(c_ref.shape[1] // LANES):
        cols = slice(h * LANES, (h + 1) * LANES)
        conv = first_ref[:, cols].astype(f32) + edge_terms(before_ref, lower_ref, h, 0)
        dq_ref[:, cols] = c_ref[:, cols] * conv.astype(bf16)


def edge_key_body(after_ref, last_ref, lower_ref, k_ref, v_ref, dk_in, dv_in, dk_ref, dv_ref):
    for h in range(k_ref.shape[1] // LANES):
        cols = slice(h * LANES, (h + 1) * LANES)
        back = (last_ref[:, cols].astype(f32) + edge_terms(after_ref, lower_ref, h, 1)).astype(bf16)
        dk_ref[:, cols] = v_ref[:, cols] * back
        dv_ref[:, cols] = k_ref[:, cols] * back


def edge_outputs(body, tail, halo, inner, lower, factors, grads, wide):
    length, width = grads[0].shape
    span = lower.shape[1]
    place = length // span - 1 if tail else 0
    head = pl.BlockSpec((span, wide), lambda i: (0, i))
    edge = pl.BlockSpec((span, wide), lambda i: (place, i))
    some = pl.BlockSpec((wide * lower.shape[0] // width, span, span), lambda i: (i, 0, 0))
    count, ahead = len(grads), 3 + len(factors)
    return pl.pallas_call(
        body,
        grid=(width // wide,),
        in_specs=[head, head, some] + [edge] * len(factors) + [pl.BlockSpec(memory_space=pl.ANY)] * count,
        out_specs=[edge] * count,
        out_shape=[jax.ShapeDtypeStruct(g.shape, bf16) for g in grads],
        input_output_aliases={ahead + i: i for i in range(count)},
        compiler_params=pltpu.CompilerParams(vmem_limit_bytes=EDGE_VMEM),
        cost_estimate=pl.CostEstimate(flops=2 * span * span * width, bytes_accessed=12 * span * width, transcendentals=0),
    )(halo, inner, lower, *factors, *grads)


def norm_body(inverse, own_ref, *refs):
    out_ref, squares_ref = refs[-2:]
    own = (own_ref[...] + refs[0][...]) * inverse
    total = jnp.sum(own * own)
    if len(refs) == 5:
        other = (refs[1][...] + refs[2][...]) * inverse
        total = total + jnp.sum(other * other)
    out_ref[...] = own
    squares_ref[...] = jnp.full(squares_ref.shape, total, f32)


def scale_body(limit, scaled_ref, *refs):
    out_ref = refs[-1]
    squares = refs[0][...]
    for ref in refs[1:-1]:
        squares = squares + ref[...]
    factor = jnp.minimum(1.0, limit / jnp.sqrt(squares[:1] + epsilon))
    flip = (lax.broadcasted_iota(jnp.int32, (LANES, LANES), 0) + lax.broadcasted_iota(jnp.int32, (LANES, LANES), 1)) % LANES == 0
    out_ref[...] = jnp.dot(scaled_ref[...] * factor, flip.astype(f32), precision=lax.Precision.HIGHEST, preferred_element_type=f32)


def small_call(body, out_shape, *args):
    return pl.pallas_call(body, out_shape=out_shape, compiler_params=pltpu.CompilerParams(vmem_limit_bytes=8 << 20))(*args)


def on_device(query_in, key_in, value_in, cotangent, filter_taps):
    length, width = query_in.shape
    local_groups, span = filter_taps.shape
    group_size = width // local_groups
    across, along = lax.axis_size("ctx"), lax.axis_size("tp")
    inverse = 1.0 / math.sqrt(length * across * group_size)
    limit = clip_ratio * math.sqrt(local_groups * along * span)
    after = shifted(cotangent[:span] * query_in[:span], "ctx", -1)
    before = shifted(key_in[length - span :] * value_in[length - span :], "ctx", 1)
    query_grad, key_grad, value_grad, inner, first, last, lower = main_part(query_in, key_in, value_in, cotangent, filter_taps)
    wide = min(width, 1024)
    raw = edge_raw(key_in, value_in, after, inner, wide)
    query_grad, = edge_outputs(edge_query_body, False, before, first, lower, [cotangent], [query_grad], wide)
    key_grad, value_grad = edge_outputs(edge_key_body, True, after, last, lower, [key_in, value_in], [key_grad, value_grad], wide)
    for masks in rounds(powers(2, across)):
        received = partners(raw, [(m, 0) for m in masks])
        if masks[0] == 2:
            *received, query_grad = lax.optimization_barrier((*received, query_grad))
        raw = summed(raw, received)
    masks = [(1, 0), (0, 2), (1, 2)] if along > 2 else [(1, 0)]
    shapes = (jax.ShapeDtypeStruct(raw.shape, f32), jax.ShapeDtypeStruct((8, LANES), f32))
    *received, key_grad, value_grad = lax.optimization_barrier((*partners(raw, masks), key_grad, value_grad))
    scaled, squares = small_call(lambda *refs: norm_body(inverse, *refs), shapes, raw, *received)
    steps = [1] + powers(4, along)
    for step in steps[:-1]:
        squares = squares + partners(squares, [(0, step)])[0]
    filter_grad = small_call(lambda *refs: scale_body(limit, *refs), shapes[0], scaled, squares, *partners(squares, [(0, steps[-1])]))
    return (query_grad, key_grad, value_grad, filter_grad)


def solution(mesh):
    placed = (P("ctx", "tp"), P("ctx", "tp"), P("ctx", "tp"), P("ctx", "tp"), P("tp", None))
    return jax.shard_map(
        on_device,
        mesh=mesh,
        in_specs=placed,
        out_specs=(P("ctx", "tp"), P("ctx", "tp"), P("ctx", "tp"), P("tp", None)),
        check_vma=False,
    )
```

```python
import math

import jax
import jax.numpy as jnp
from jax import lax
from jax.experimental import pallas as pl
from jax.experimental.pallas import tpu as pltpu
from jax.sharding import PartitionSpec as P

clip_ratio = 0.25
epsilon = 1e-06
LANES = 128
TILE = 16
WIDE = 256
CHUNK = 2
VMEM = 127 << 19
EDGE_VMEM = 61 << 20
bf16 = jnp.bfloat16
f32 = jnp.float32


def shifted(value, axis, steps):
    count = lax.axis_size(axis)
    first, last = max(0, -steps), min(count, count - steps)
    return lax.ppermute(value, axis, [(source, source + steps) for source in range(first, last)])


def partners(value, masks):
    across, along = lax.axis_size("ctx"), lax.axis_size("tp")
    numbers = range(across * along)
    return [lax.ppermute(value, ("ctx", "tp"), [(i, i ^ (c * along + t)) for i in numbers]) for c, t in masks]


def summed(value, received):
    if len(received) == 1:
        return value + received[0]
    return (value + received[0]) + (received[1] + received[2])


def rounds(bits):
    out = []
    while bits:
        a, b, bits = bits[0], bits[1] if len(bits) > 1 else 0, bits[2:]
        out.append([a, b, a ^ b] if b else [a])
    return out


def powers(lowest, count):
    out = []
    while lowest < count:
        out.append(lowest)
        lowest *= 2
    return out


def toeplitz(tap):
    lane = lax.broadcasted_iota(jnp.int32, (TILE, LANES), 1)
    row = lax.broadcasted_iota(jnp.int32, (TILE, LANES), 0)
    zero = jnp.zeros((TILE, LANES), bf16)
    tap = jnp.broadcast_to(tap.astype(bf16).astype(f32), (TILE, LANES))
    first = pltpu.roll(tap, 0, 1, stride=1, stride_axis=0).astype(bf16)
    upper, lower = [], []
    for a in range(LANES // TILE):
        rows = pltpu.roll(first, a * TILE, 1) if a else first
        keep = lane >= row + a * TILE
        upper.append(jnp.where(keep, rows, zero))
        lower.append(jnp.where(keep, zero, rows))
    return jnp.concatenate(upper, 0), jnp.concatenate(lower, 0)


def diagonal_shifts():
    source = lax.broadcasted_iota(jnp.int32, (LANES, LANES), 0)
    target = lax.broadcasted_iota(jnp.int32, (LANES, LANES), 1)
    return jnp.concatenate([((source + target) % LANES == a).astype(bf16) for a in range(0, LANES, TILE)], 0)


def diagonal_sums(folded, shifts, first, groups):
    at = slice(first * TILE, (first + groups) * TILE)
    left = jnp.concatenate([folded[a, at, :] for a in range(LANES // TILE)], 1)
    total = jnp.dot(left, shifts, preferred_element_type=f32)
    sums = []
    for g in range(groups):
        part = pltpu.roll(total[g * TILE : (g + 1) * TILE], 0, 1, stride=1, stride_axis=0)
        sums.append(jnp.sum(part, 0, keepdims=True))
    return jnp.concatenate(sums, 0)


def main_body(q_ref, k_ref, v_ref, c_ref, taps_ref, dq_ref, dk_ref, dv_ref, folded, first_ref, last_ref, lower_ref, mt, st, ct, bt):
    length, width = q_ref.shape
    groups = taps_ref.shape[0]
    group = width // groups
    blocks = length // LANES
    lane = lax.broadcasted_iota(jnp.int32, (TILE, LANES), 1)
    row = lax.broadcasted_iota(jnp.int32, (TILE, LANES), 0)
    flat = lambda x: x.reshape(blocks * group, LANES)
    per = LANES // group
    halves = width // LANES

    def enter(h, b):
        cols, rows = slice(h * LANES, (h + 1) * LANES), slice(b * LANES, (b + 1) * LANES)
        mixed = k_ref[rows, cols] * v_ref[rows, cols]
        mt[h, b + 1] = mixed.T
        st[h, b] = (c_ref[rows, cols] * q_ref[rows, cols]).T

    def convolve(h, p):
        g = h * per + p
        own = slice(p * group, (p + 1) * group)
        upper, lower = toeplitz(taps_ref[g : g + 1, :])
        lower_ref[g] = lower
        mixed = flat(mt[h, 1 : blocks + 1, own, :])
        window = jnp.concatenate([flat(mt[h, :blocks, own, :]), mixed], 1)
        ahead = jnp.concatenate([flat(st[h, :blocks, own, :]), flat(st[h, 1 : blocks + 1, own, :])], 1)
        conv = jnp.dot(window, jnp.concatenate([lower, upper], 0), preferred_element_type=f32)
        back = lax.dot_general(ahead, jnp.concatenate([upper, lower], 1), (((1,), (1,)), ((), ())), preferred_element_type=f32)
        ct[h, :, own, :] = conv.astype(bf16).reshape(blocks, group, LANES)
        bt[h, :, own, :] = back.astype(bf16).reshape(blocks, group, LANES)
        gram = lax.dot_general(mixed, ahead, (((0,), (0,)), ((), ())), preferred_element_type=f32)
        for a in range(LANES // TILE):
            rows = slice(a * TILE, (a + 1) * TILE)
            kept = jnp.where(lane >= row + a * TILE, gram[rows, :LANES], gram[rows, LANES:])
            folded[a, g * TILE : (g + 1) * TILE, :] = kept.astype(bf16)

    def leave(h, b):
        cols, rows = slice(h * LANES, (h + 1) * LANES), slice(b * LANES, (b + 1) * LANES)
        conv = ct[h, b].T
        back = bt[h, b].T
        if b == 0:
            first_ref[:, cols] = conv
        if b == blocks - 1:
            last_ref[:, cols] = back
        dq_ref[rows, cols] = c_ref[rows, cols] * conv
        dk_ref[rows, cols] = v_ref[rows, cols] * back
        dv_ref[rows, cols] = k_ref[rows, cols] * back

    share = 3
    for h in range(halves):
        mt[h, 0] = jnp.zeros((LANES, LANES), bf16)
        st[h, blocks] = jnp.zeros((LANES, LANES), bf16)
    for b in range(blocks):
        enter(0, b)
    for h in range(halves):
        for p in range(per):
            convolve(h, p)
            for b in range(p * share, min(blocks, (p + 1) * share)):
                if h + 1 < halves:
                    enter(h + 1, b)
                if h > 0:
                    leave(h - 1, b)
    for b in range(blocks):
        leave(halves - 1, b)


def main_part(q, k, v, c, taps):
    length, width = q.shape
    local_groups, span = taps.shape
    groups = WIDE * local_groups // width
    blocks, halves = length // LANES, WIDE // LANES
    block = pl.BlockSpec((length, WIDE), lambda i: (0, i))
    halo = pl.BlockSpec((span, WIDE), lambda i: (0, i))
    some = pl.BlockSpec((groups, span), lambda i: (i, 0))
    big = jax.ShapeDtypeStruct((length, width), bf16)
    edge = jax.ShapeDtypeStruct((span, width), bf16)
    return pl.pallas_call(
        main_body,
        grid=(width // WIDE,),
        in_specs=[block] * 4 + [some],
        out_specs=[block] * 3 + [pl.BlockSpec((span // TILE, groups * TILE, span), lambda i: (0, i, 0)), halo, halo, pl.BlockSpec((groups, span, span), lambda i: (i, 0, 0))],
        out_shape=[big, big, big, jax.ShapeDtypeStruct((span // TILE, local_groups * TILE, span), bf16), edge, edge, jax.ShapeDtypeStruct((local_groups, span, span), bf16)],
        scratch_shapes=[pltpu.VMEM((halves, blocks + 1, LANES, LANES), bf16)] * 2
        + [pltpu.VMEM((halves, blocks, LANES, LANES), bf16)] * 2,
        compiler_params=pltpu.CompilerParams(vmem_limit_bytes=VMEM),
        cost_estimate=pl.CostEstimate(flops=12 * length * width * LANES, bytes_accessed=14 * length * width, transcendentals=0),
    )(q, k, v, c, taps)


def edge_raw_body(k_ref, v_ref, after_ref, inner_ref, out_ref, folded):
    width = k_ref.shape[1]
    groups = out_ref.shape[0]
    group = width // groups
    lane = lax.broadcasted_iota(jnp.int32, (TILE, LANES), 1)
    row = lax.broadcasted_iota(jnp.int32, (TILE, LANES), 0)
    per = LANES // group
    zero = jnp.zeros((TILE, LANES), bf16)
    shifts = diagonal_shifts()
    chunk = CHUNK * per

    def finish(first):
        out_ref[first : first + chunk, :] = diagonal_sums(folded, shifts, first, chunk)

    for h in range(width // LANES):
        cols = slice(h * LANES, (h + 1) * LANES)
        mixed = k_ref[:, cols] * v_ref[:, cols]
        ahead = after_ref[:, cols].T
        empty = jnp.zeros((group, LANES), bf16)
        for p in range(0, per, 2):
            pick = lambda n: jnp.concatenate([ahead[i * group : (i + 1) * group] if i == n else empty for i in range(per)], 0)
            gram = jnp.dot(mixed, jnp.concatenate([pick(p), pick(p + 1)], 1), preferred_element_type=f32)
            for n in range(2):
                g = h * per + p + n
                at = slice(g * TILE, (g + 1) * TILE)
                for a in range(LANES // TILE):
                    part = gram[a * TILE : (a + 1) * TILE, n * LANES : (n + 1) * LANES].astype(bf16)
                    folded[a, at, :] = inner_ref[a, at, :] + jnp.where(lane < row + a * TILE, part, zero)
        if h % CHUNK == 0 and h >= CHUNK:
            finish((h - CHUNK) * per)
    finish(groups - chunk)


def edge_raw(k, v, after, inner, wide):
    length, width = k.shape
    span = inner.shape[2]
    local_groups = inner.shape[1] // TILE
    groups = wide * local_groups // width
    tail = pl.BlockSpec((span, wide), lambda i: (length // span - 1, i))
    halo = pl.BlockSpec((span, wide), lambda i: (0, i))
    return pl.pallas_call(
        edge_raw_body,
        grid=(width // wide,),
        in_specs=[tail, tail, halo, pl.BlockSpec((span // TILE, groups * TILE, span), lambda i: (0, i, 0))],
        out_specs=pl.BlockSpec((groups, span), lambda i: (i, 0)),
        out_shape=jax.ShapeDtypeStruct((local_groups, span), f32),
        scratch_shapes=[pltpu.VMEM((LANES // TILE, groups * TILE, LANES), bf16)],
        compiler_params=pltpu.CompilerParams(vmem_limit_bytes=EDGE_VMEM),
        cost_estimate=pl.CostEstimate(flops=2 * span * span * width, bytes_accessed=14 * span * width, transcendentals=0),
    )(k, v, after, inner)


def edge_terms(halo_ref, lower_ref, h, side):
    group = halo_ref.shape[1] // lower_ref.shape[0]
    per = LANES // group
    far = halo_ref[:, h * LANES : (h + 1) * LANES].T
    parts = []
    for p in range(per):
        dims = (((1,), (side,)), ((), ()))
        parts.append(lax.dot_general(far[p * group : (p + 1) * group], lower_ref[h * per + p], dims, preferred_element_type=f32))
    return jnp.concatenate(parts, 0).astype(bf16).T.astype(f32)


def edge_query_body(before_ref, first_ref, lower_ref, c_ref, dq_in, dq_ref):
    for h in range(c_ref.shape[1] // LANES):
        cols = slice(h * LANES, (h + 1) * LANES)
        conv = first_ref[:, cols].astype(f32) + edge_terms(before_ref, lower_ref, h, 0)
        dq_ref[:, cols] = c_ref[:, cols] * conv.astype(bf16)


def edge_key_body(after_ref, last_ref, lower_ref, k_ref, v_ref, dk_in, dv_in, dk_ref, dv_ref):
    for h in range(k_ref.shape[1] // LANES):
        cols = slice(h * LANES, (h + 1) * LANES)
        back = (last_ref[:, cols].astype(f32) + edge_terms(after_ref, lower_ref, h, 1)).astype(bf16)
        dk_ref[:, cols] = v_ref[:, cols] * back
        dv_ref[:, cols] = k_ref[:, cols] * back


def edge_outputs(body, tail, halo, inner, lower, factors, grads, wide):
    length, width = grads[0].shape
    span = lower.shape[1]
    place = length // span - 1 if tail else 0
    head = pl.BlockSpec((span, wide), lambda i: (0, i))
    edge = pl.BlockSpec((span, wide), lambda i: (place, i))
    some = pl.BlockSpec((wide * lower.shape[0] // width, span, span), lambda i: (i, 0, 0))
    count, ahead = len(grads), 3 + len(factors)
    return pl.pallas_call(
        body,
        grid=(width // wide,),
        in_specs=[head, head, some] + [edge] * len(factors) + [pl.BlockSpec(memory_space=pl.ANY)] * count,
        out_specs=[edge] * count,
        out_shape=[jax.ShapeDtypeStruct(g.shape, bf16) for g in grads],
        input_output_aliases={ahead + i: i for i in range(count)},
        compiler_params=pltpu.CompilerParams(vmem_limit_bytes=EDGE_VMEM),
        cost_estimate=pl.CostEstimate(flops=2 * span * span * width, bytes_accessed=12 * span * width, transcendentals=0),
    )(halo, inner, lower, *factors, *grads)


def norm_body(inverse, own_ref, *refs):
    out_ref, squares_ref = refs[-2:]
    own = (own_ref[...] + refs[0][...]) * inverse
    total = jnp.sum(own * own)
    if len(refs) == 5:
        other = (refs[1][...] + refs[2][...]) * inverse
        total = total + jnp.sum(other * other)
    out_ref[...] = own
    squares_ref[...] = jnp.full(squares_ref.shape, total, f32)


def scale_body(limit, scaled_ref, *refs):
    out_ref = refs[-1]
    squares = refs[0][...]
    for ref in refs[1:-1]:
        squares = squares + ref[...]
    factor = jnp.minimum(1.0, limit / jnp.sqrt(squares[:1] + epsilon))
    flip = (lax.broadcasted_iota(jnp.int32, (LANES, LANES), 0) + lax.broadcasted_iota(jnp.int32, (LANES, LANES), 1)) % LANES == 0
    out_ref[...] = jnp.dot(scaled_ref[...] * factor, flip.astype(f32), precision=lax.Precision.HIGHEST, preferred_element_type=f32)


def small_call(body, out_shape, *args):
    return pl.pallas_call(body, out_shape=out_shape, compiler_params=pltpu.CompilerParams(vmem_limit_bytes=8 << 20))(*args)


def on_device(query_in, key_in, value_in, cotangent, filter_taps):
    length, width = query_in.shape
    local_groups, span = filter_taps.shape
    group_size = width // local_groups
    across, along = lax.axis_size("ctx"), lax.axis_size("tp")
    inverse = 1.0 / math.sqrt(length * across * group_size)
    limit = clip_ratio * math.sqrt(local_groups * along * span)
    signal, mixed = lax.optimization_barrier((cotangent[:span] * query_in[:span], key_in[length - span :] * value_in[length - span :]))
    after = shifted(signal, "ctx", -1)
    before = shifted(mixed, "ctx", 1)
    query_grad, key_grad, value_grad, inner, first, last, lower = main_part(query_in, key_in, value_in, cotangent, filter_taps)
    wide = min(width, 1024)
    raw = edge_raw(key_in, value_in, after, inner, wide)
    query_grad, = edge_outputs(edge_query_body, False, before, first, lower, [cotangent], [query_grad], wide)
    key_grad, value_grad = edge_outputs(edge_key_body, True, after, last, lower, [key_in, value_in], [key_grad, value_grad], wide)
    for masks in rounds(powers(2, across)):
        received = partners(raw, [(m, 0) for m in masks])
        if masks[0] == 2:
            *received, key_grad, value_grad = lax.optimization_barrier((*received, key_grad, value_grad))
        raw = summed(raw, received)
    masks = [(1, 0), (0, 2), (1, 2)] if along > 2 else [(1, 0)]
    shapes = (jax.ShapeDtypeStruct(raw.shape, f32), jax.ShapeDtypeStruct((8, LANES), f32))
    *received, query_grad = lax.optimization_barrier((*partners(raw, masks), query_grad))
    scaled, squares = small_call(lambda *refs: norm_body(inverse, *refs), shapes, raw, *received)
    steps = [1] + powers(4, along)
    for step in steps[:-1]:
        squares = squares + partners(squares, [(0, step)])[0]
    filter_grad = small_call(lambda *refs: scale_body(limit, *refs), shapes[0], scaled, squares, *partners(squares, [(0, steps[-1])]))
    return (query_grad, key_grad, value_grad, filter_grad)


def solution(mesh):
    placed = (P("ctx", "tp"), P("ctx", "tp"), P("ctx", "tp"), P("ctx", "tp"), P("tp", None))
    return jax.shard_map(
        on_device,
        mesh=mesh,
        in_specs=placed,
        out_specs=(P("ctx", "tp"), P("ctx", "tp"), P("ctx", "tp"), P("tp", None)),
        check_vma=False,
    )
```
